32 devices in a mesh: groups: 2 (over y), dom: 4 (over z), feat: 2 (over x), sub: 2 (over core).
Axes of the slice: x: 2, y: 2, z: 4, core: 2. Of those that a mesh axis runs over, the one named last changes fastest.
Arguments:
- grid_latent: bfloat16 [16384, 512], P(('groups', 'dom')), parts along dimension 0, may hold values from -6 to 6
- mesh_latent: bfloat16 [6144, 512], P(('groups', 'dom'), 'feat'), parts along dimension 0, may hold values from -6 to 6
- encoder_tiles: int32 [2, 256], P(None, ('dom', 'sub')), may hold values from 0 to 31, as said below
- encoder_lanes: int32 [16384], P(('dom', 'sub')), may hold values from 0 to 63, as said below
- encoder_geometry: float32 [4, 16384], P(None, ('dom', 'sub')), may hold values from -6 to 6
- halo_tiles: int32 [4, 4, 3], P('dom'), may hold values from -1 to 11, as said below
- mesh_tiles: int32 [2, 192], P(None, ('dom', 'sub')), may hold values from 0 to 23, as said below
- mesh_lanes: int32 [12288], P(('dom', 'sub')), may hold values from 0 to 63, as said below
- mesh_geometry: float32 [4, 12288], P(None, ('dom', 'sub')), may hold values from -6 to 6
- sender_weight: bfloat16 [3, 512, 512], P(None, None, 'feat'), may hold values from -0.25 to 0.25
- receiver_weight: bfloat16 [3, 512, 512], P(None, None, 'feat'), may hold values from -0.25 to 0.25
- node_weight: bfloat16 [3, 512, 512], P(None, None, 'feat'), may hold values from -0.25 to 0.25
- edge_weight: float32 [3, 4, 512], P(None, None, 'feat'), may hold values from -3 to 3
- edge_bias: float32 [3, 512], P(None, 'feat'), may hold values from -3 to 3
- node_bias: float32 [3, 512], P(None, 'feat'), may hold values from -3 to 3
- output_weight: bfloat16 [3, 512, 512], P(None, None, 'feat'), may hold values from -4 to 4
- norm_gain: float32 [3, 512], P(None, 'feat'), may hold values from 0.1 to 1.9
Outputs:
- mesh_out: bfloat16 [6144, 512], P(('groups', 'dom'), 'feat'), parts along dimension 0
The draws below stay inside these ranges and needn't reach their ends.
There are 2 independent parts, one for each index of `groups`. The reference program is written for one: setup_inputs(seed, part) draws one part's arguments, and reference() takes and returns one part's arrays. A program takes and returns all parts, laid end to end along the dimension named above; an argument that names none is the same for every part. Nothing has to cross between parts.
Inputs may be any that keep to these rules, and one draw needn't show every extreme that they name: `encoder_tiles`: row 0 names source grid tiles below 32, each tile of a partition named by exactly 2 of its blocks; row 1 names destination mesh tiles below 12, each named at least once in a partition. Partition p's blocks are those that dom index p holds. `encoder_lanes`: the lanes of one block are a permutation of 0 .. 63. `halo_tiles`: entry [p, q, c] is the c-th mesh tile that partition p sends to partition q, a tile below 12, or -1 for an empty slot. Only q = p + 1, q = p - 1 and q = p + 4 // 2 modulo 4 hold tiles; a list's tiles are distinct and fill its first slots; each such list holds at least one tile, and some list holds 3 in every draw. `mesh_tiles`: row 0: a source below M = 12 is a local tile; a larger one s names slot (s - M) % 3 of the list that partition (s - M) // 3 sends to this partition, always a filled slot, and every filled slot is named by exactly one block of the receiving partition; every local tile is named at least once. Row 1: destination tiles, each named by exactly 4 blocks of the partition. `mesh_lanes`: the lanes of one block are a permutation of 0 .. 63.
All inputs are finite; a program needn't handle non-finite values.
Results may differ from the reference program's by a relative error of at most 0.0064.
Values may be sent and summed in bfloat16 or wider, within the bound.
A program may use at most 64 MiB of HBM per device.

```python
import math
import jax
import jax.numpy as jnp
from jax import lax

D = 512
HID = 512
TILE = 64
EDGE_FAN = 2
MESH_FAN = 4
GRID_DEV = 2048
MESH_DEV = 768
LAYERS = 3
CAP = 3
GRID = 8192
MESH = 3072
G2M_BLOCKS = 256
M_BLOCKS = 192
G2M_EDGES = 16384
M_EDGES = 12288
N_DOM = 4


def tile_orders(key, count, length):
    key_list = jax.random.split(key, count)
    return jax.vmap(lambda single: jax.random.permutation(single, length))(key_list).astype(jnp.int32)


def halo_plan(key):
    key_list = jax.random.split(key, 6)
    mesh_count = MESH_DEV // TILE
    forward_count = jax.random.randint(key_list[0], (N_DOM,), 1, CAP + 1, dtype=jnp.int32).at[0].set(CAP)
    backward_count = jax.random.randint(key_list[1], (N_DOM,), 1, CAP + 1, dtype=jnp.int32).at[N_DOM - 1].set(CAP)
    far_count = jax.random.randint(key_list[4], (N_DOM,), 1, CAP + 1, dtype=jnp.int32).at[1].set(CAP)
    forward_tiles = tile_orders(key_list[2], N_DOM, mesh_count)[:, :CAP]
    forward_tiles = forward_tiles.at[0].set(mesh_count - 1 - jnp.arange(CAP, dtype=jnp.int32))
    backward_tiles = tile_orders(key_list[3], N_DOM, mesh_count)[:, :CAP]
    far_tiles = tile_orders(key_list[5], N_DOM, mesh_count)[:, :CAP]
    return (forward_count, backward_count, far_count, forward_tiles, backward_tiles, far_tiles)


def draw_encoder_tiles(key, part):
    key = jax.random.fold_in(key, 11)
    first_key, second_key = jax.random.split(key)
    grid_count = GRID_DEV // TILE
    mesh_count = MESH_DEV // TILE
    per_part = EDGE_FAN * grid_count
    source = tile_orders(first_key, N_DOM, per_part) % grid_count
    target = tile_orders(second_key, N_DOM, per_part) % mesh_count
    return jnp.stack([source.reshape(-1), target.reshape(-1)]).astype(jnp.int32)


def draw_encoder_lanes(key, part):
    key = jax.random.fold_in(key, 12)
    return tile_orders(key, G2M_BLOCKS, TILE).reshape(-1)


def draw_halo_tiles(key, part):
    forward_count, backward_count, far_count, forward_tiles, backward_tiles, far_tiles = halo_plan(key)
    sender = jnp.arange(N_DOM, dtype=jnp.int32)[:, None, None]
    peer_part = jnp.arange(N_DOM, dtype=jnp.int32)[None, :, None]
    slot_index = jnp.arange(CAP, dtype=jnp.int32)[None, None, :]
    forward_value = jnp.where(slot_index < forward_count[:, None, None], forward_tiles[:, None, :], -1)
    backward_value = jnp.where(slot_index < backward_count[:, None, None], backward_tiles[:, None, :], -1)
    far_value = jnp.where(slot_index < far_count[:, None, None], far_tiles[:, None, :], -1)
    listing = jnp.where(peer_part == (sender + 1) % N_DOM, forward_value, jnp.where(peer_part == (sender + N_DOM - 1) % N_DOM, backward_value, jnp.where(peer_part == (sender + N_DOM // 2) % N_DOM, far_value, -1)))
    return listing.astype(jnp.int32)


def draw_mesh_tiles(key, part):
    forward_count, backward_count, far_count, unused_forward, unused_backward, unused_far = halo_plan(key)
    key = jax.random.fold_in(key, 14)
    key_list = jax.random.split(key, 3)
    mesh_count = MESH_DEV // TILE
    per_part = MESH_FAN * mesh_count
    owner_part = jnp.arange(N_DOM, dtype=jnp.int32)[:, None]
    column = jnp.arange(per_part, dtype=jnp.int32)[None, :]
    previous = (owner_part + N_DOM - 1) % N_DOM
    following = (owner_part + 1) % N_DOM
    opposite = (owner_part + N_DOM // 2) % N_DOM
    filler = jax.random.randint(key_list[0], (N_DOM, per_part), 0, mesh_count, dtype=jnp.int32)
    from_previous = (column < CAP) & (column < forward_count[previous])
    from_following = (column >= CAP) & (column < 2 * CAP) & (column - CAP < backward_count[following])
    from_opposite = (column >= 2 * CAP) & (column < 3 * CAP) & (column - 2 * CAP < far_count[opposite])
    local_run = (column >= 3 * CAP) & (column < 3 * CAP + mesh_count)
    candidate = jnp.where(from_previous, mesh_count + previous * CAP + column, jnp.where(from_following, mesh_count + following * CAP + column - CAP, jnp.where(from_opposite, mesh_count + opposite * CAP + column - 2 * CAP, jnp.where(local_run, column - 3 * CAP, filler))))
    shuffle = tile_orders(key_list[1], N_DOM, per_part)
    source = jnp.take_along_axis(candidate, shuffle, axis=1)
    target = tile_orders(key_list[2], N_DOM, per_part) % mesh_count
    return jnp.stack([source.reshape(-1), target.reshape(-1)]).astype(jnp.int32)


def draw_mesh_lanes(key, part):
    key = jax.random.fold_in(key, 15)
    return tile_orders(key, M_BLOCKS, TILE).reshape(-1)


def draw_output_weight(key, part):
    key = jax.random.fold_in(key, 16)
    entry_key, scale_key = jax.random.split(key)
    column = jnp.arange(D, dtype=jnp.float32) / D
    spread = jax.random.uniform(scale_key, (D,), jnp.float32)
    entries = jnp.clip(jax.random.normal(entry_key, (LAYERS, HID, D), jnp.float32), -4.0, 4.0)
    col_scale = jnp.exp(math.log(3.0) * column + math.log(10.0) * spread)
    return (entries * col_scale * 0.01).astype(jnp.bfloat16)


def shard_levels(stream_key, shape, shards, least, largest):
    def one(axis_at, parts):
        steps = jax.random.uniform(jax.random.fold_in(jax.random.fold_in(stream_key, 6), axis_at), (parts,), jnp.float32, least / len(shards), largest / len(shards))
        return jnp.repeat(jnp.exp(steps), shape[axis_at] // parts).reshape((-1,) + (1,) * (len(shape) - axis_at - 1))

    level = one(*shards[0])
    for cut in shards[1:]:
        level = level * one(*cut)
    return level


def bell_draw(own_key, shape, width, most, cuts=(), kind=jnp.bfloat16):
    array = jax.random.normal(own_key, shape, jnp.float32) * width
    if len(cuts) > 0:
        array = shard_levels(own_key, shape, cuts, -0.22, 0.18) * array
    return jnp.clip(array, min=-most, max=most).astype(kind)


def setup_inputs(seed: int = 0, part: int = 0) -> dict:
    arg_keys = jax.random.split(jax.random.key(seed), 18)
    part_splits = jax.random.split(jax.random.fold_in(arg_keys[17], part), 18)
    return {
        "grid_latent": bell_draw(part_splits[0], (GRID, D), 1.0, 6.0, ((0, 4),)),
        "mesh_latent": bell_draw(part_splits[1], (MESH, D), 1.0, 6.0, ((0, 4), (1, 2))),
        "encoder_tiles": draw_encoder_tiles(jax.random.fold_in(arg_keys[17], 71), part),
        "encoder_lanes": draw_encoder_lanes(jax.random.fold_in(arg_keys[17], 71), part),
        "encoder_geometry": bell_draw(arg_keys[4], (4, G2M_EDGES), 1.0, 6.0, ((1, 8),), jnp.float32),
        "halo_tiles": draw_halo_tiles(jax.random.fold_in(arg_keys[17], 71), part),
        "mesh_tiles": draw_mesh_tiles(jax.random.fold_in(arg_keys[17], 71), part),
        "mesh_lanes": draw_mesh_lanes(jax.random.fold_in(arg_keys[17], 71), part),
        "mesh_geometry": bell_draw(arg_keys[8], (4, M_EDGES), 1.0, 6.0, ((1, 8),), jnp.float32),
        "sender_weight": bell_draw(arg_keys[9], (LAYERS, D, HID), D ** -0.5, 0.25, ((2, 2),)),
        "receiver_weight": bell_draw(arg_keys[10], (LAYERS, D, HID), D ** -0.5, 0.25, ((2, 2),)),
        "node_weight": bell_draw(arg_keys[11], (LAYERS, D, HID), D ** -0.5, 0.25, ((2, 2),)),
        "edge_weight": bell_draw(arg_keys[12], (LAYERS, 4, HID), 4 ** -0.5, 3.0, ((2, 2),), jnp.float32),
        "edge_bias": bell_draw(arg_keys[13], (LAYERS, HID), 0.5, 3.0, ((1, 2),), jnp.float32),
        "node_bias": bell_draw(arg_keys[14], (LAYERS, HID), 0.5, 3.0, ((1, 2),), jnp.float32),
        "output_weight": draw_output_weight(jax.random.fold_in(arg_keys[17], 71), part),
        "norm_gain": jnp.clip(1.0 + 0.18 * jax.random.normal(arg_keys[16], (LAYERS, D), jnp.float32), 0.1, 1.9),
    }


def reference(grid_latent, mesh_latent, encoder_tiles, encoder_lanes, encoder_geometry, halo_tiles, mesh_tiles, mesh_lanes, mesh_geometry, sender_weight, receiver_weight, node_weight, edge_weight, edge_bias, node_bias, output_weight, norm_gain):
    band_share = GRID_DEV // N_DOM
    grid_sorted = grid_latent.reshape(N_DOM, N_DOM, band_share, D).transpose(1, 0, 2, 3).reshape(GRID, D)
    tile_count = MESH_DEV // TILE
    lane_index = jnp.arange(TILE, dtype=jnp.int32)
    latent = mesh_latent
    for layer_index in range(LAYERS):
        receivers = jnp.dot(latent, receiver_weight[layer_index], preferred_element_type=jnp.float32)
        base_term = jnp.dot(latent, node_weight[layer_index], preferred_element_type=jnp.float32)
        if layer_index == 0:
            sender_table = jnp.dot(grid_sorted, sender_weight[0], preferred_element_type=jnp.float32)
            tile_pairs = encoder_tiles
            lane_list = encoder_lanes
            geometry = encoder_geometry
            blocks = tile_pairs.shape[1]
            owner_part = jnp.arange(blocks, dtype=jnp.int32) // (blocks // N_DOM)
            first_row = owner_part * GRID_DEV + TILE * tile_pairs[0]
        else:
            sender_table = jnp.dot(latent, sender_weight[layer_index], preferred_element_type=jnp.float32).astype(jnp.bfloat16)
            tile_pairs = mesh_tiles
            lane_list = mesh_lanes
            geometry = mesh_geometry
            blocks = tile_pairs.shape[1]
            owner_part = jnp.arange(blocks, dtype=jnp.int32) // (blocks // N_DOM)
            source_tile = tile_pairs[0]
            shifted = jnp.maximum(source_tile - tile_count, 0)
            sender_part = shifted // CAP
            slot_index = shifted % CAP
            remote_tile = jnp.maximum(halo_tiles[sender_part, owner_part, slot_index], 0)
            first_row = jnp.where(source_tile < tile_count, owner_part * MESH_DEV + TILE * source_tile, sender_part * MESH_DEV + TILE * remote_tile)
        source_rows = (first_row[:, None] + lane_list.reshape(blocks, TILE)).reshape(-1)
        target_rows = ((owner_part * MESH_DEV + TILE * tile_pairs[1])[:, None] + lane_index[None, :]).reshape(-1)
        geometry_term = jnp.einsum('ce,ch->eh', geometry, edge_weight[layer_index], precision=lax.Precision.HIGHEST)
        before = geometry_term + sender_table[source_rows].astype(jnp.float32) + receivers[target_rows] + edge_bias[layer_index]
        message = jax.nn.silu(before)
        gathered = jax.ops.segment_sum(message, target_rows, num_segments=MESH)
        hidden = jax.nn.silu(base_term + gathered + node_bias[layer_index]).astype(jnp.bfloat16)
        update = jnp.dot(hidden, output_weight[layer_index], preferred_element_type=jnp.float32)
        row_mean = lax.optimization_barrier(jnp.sum(update, axis=1)) / D
        variance = lax.optimization_barrier(jnp.sum(update * update, axis=1)) / D - row_mean * row_mean
        normed = (update - row_mean[:, None]) * lax.rsqrt(variance + 1e-05)[:, None] * norm_gain[layer_index]
        latent = (latent.astype(jnp.float32) + normed).astype(jnp.bfloat16)
    return latent
```

```python
import functools

import jax
import jax.numpy as jnp
from jax import lax
from jax.experimental import pallas as pl
from jax.experimental.pallas import tpu as pltpu
from jax.sharding import PartitionSpec as P

TILE = 64
LAYERS = 3
CAP = 3
EPSILON = 1e-05
DEVICE_MESH = pl.DeviceIdType.MESH
F32 = jnp.float32
BF16 = jnp.bfloat16


def silu(value):
    half = 0.5 * value
    return half + half * jnp.tanh(half)


def contract_rows(left, right, precision=None):
    return lax.dot_general(
        left, right, (((0,), (0,)), ((), ())), preferred_element_type=F32, precision=precision
    )


def plan_kernel(n_dom, tile_count, encoder_tiles, mesh_tiles, halo_tiles, plan, last):
    dom = lax.axis_index("dom")
    previous = lax.rem(dom + n_dom - 1, n_dom)
    following = lax.rem(dom + 1, n_dom)

    def chain(tiles, row):
        blocks = tiles.shape[1]

        def clear(t, carry):
            last[t] = blocks
            return carry

        def follow(block, carry):
            target = tiles[1, block]
            plan[row + 1, block] = last[target]
            plan[row + 3, block] = target
            last[target] = block
            return carry

        def keep(t, carry):
            plan[row + 2, t] = last[t]
            return carry

        lax.fori_loop(0, tile_count, clear, 0)
        lax.fori_loop(0, blocks, follow, 0)
        lax.fori_loop(0, tile_count, keep, 0)

    def grid_place(block, carry):
        plan[0, block] = encoder_tiles[0, block]
        return carry

    def mesh_place(block, carry):
        tile = mesh_tiles[0, block]
        beyond = jnp.maximum(tile - tile_count, 0)
        owner = lax.div(beyond, CAP)
        slot = lax.rem(beyond, CAP)
        way = jnp.where(owner == previous, 0, jnp.where(owner == following, 1, 2))
        plan[4, block] = jnp.where(tile < tile_count, tile, tile_count + CAP * way + slot)
        return carry

    lax.fori_loop(0, encoder_tiles.shape[1], grid_place, 0)
    lax.fori_loop(0, mesh_tiles.shape[1], mesh_place, 0)
    chain(encoder_tiles, 0)
    chain(mesh_tiles, 4)
    for way, step in enumerate((1, n_dom - 1, n_dom // 2)):
        peer = lax.rem(dom + step, n_dom)
        for slot in range(CAP):
            plan[8, CAP * way + slot] = jnp.maximum(halo_tiles[0, peer, slot], 0)


def kernel(
    sizes,
    plan,
    encoder_lanes,
    mesh_lanes,
    encoder_geometry,
    mesh_geometry,
    edge_weight,
    edge_bias,
    node_bias,
    grid_latent,
    mesh_latent,
    sender_weight,
    receiver_weight,
    node_weight,
    output_weight,
    norm_gain,
    out,
    grid_half,
    sender_w,
    receiver_w,
    node_w,
    output_w,
    gain,
    grid_out,
    grid_table,
    latents,
    first_table,
    second_table,
    local_table,
    halo_out,
    receivers,
    base,
    terms_enc,
    terms_mesh,
    sums,
    share_out,
    share_in,
    hidden,
    fetch_sem,
    send_sem,
    recv_sem,
):
    n_dom, n_feat = sizes
    dom = lax.axis_index("dom")
    feat = lax.axis_index("feat")
    sub = lax.axis_index("sub")
    width = base.shape[2]
    mesh_rows = latents.shape[2]
    tile_count = mesh_rows // TILE
    half_tiles = tile_count // 2
    half_rows = mesh_rows // 2
    part_rows = half_rows // n_feat
    half_band = grid_half.shape[1]
    model_width = grid_half.shape[2]
    half_model = model_width // 2
    half_tile = TILE // 2
    half_units = half_band // half_tile

    tables = (first_table, second_table)
    fetches = []
    sends = []

    def fetch(source, target):
        copy = pltpu.make_async_copy(source, target, fetch_sem.at[len(fetches)])
        copy.start()
        fetches.append(copy)
        return copy

    def send(source, target, device):
        slot = len(sends)
        copy = pltpu.make_async_remote_copy(
            src_ref=source,
            dst_ref=target,
            send_sem=send_sem.at[slot],
            recv_sem=recv_sem.at[slot],
            device_id=device,
            device_id_type=DEVICE_MESH,
        )
        copy.start()
        sends.append(copy)
        return copy

    sibling = {"sub": 1 - sub}
    own_rows = pl.ds(pl.multiple_of(sub * half_rows, half_rows), half_rows)

    got_grid = fetch(
        grid_latent.at[:, pl.ds(pl.multiple_of(sub * half_band, half_band), half_band), :], grid_half
    )
    got_sender = fetch(sender_weight, sender_w)
    got_latent = fetch(mesh_latent, latents.at[0, feat])
    got_receiver = fetch(receiver_weight, receiver_w)
    got_node = fetch(node_weight, node_w)
    got_output = fetch(output_weight, output_w.at[feat])
    got_gain = fetch(norm_gain, gain.at[feat])

    barrier = pltpu.get_barrier_semaphore()
    dom_peers = [lax.rem(dom + step, n_dom) for step in range(1, n_dom)]
    feat_peers = [lax.rem(feat + step, n_feat) for step in range(1, n_feat)]
    feat_sources = [lax.rem(feat + n_feat - step, n_feat) for step in range(1, n_feat)]
    for peer in dom_peers:
        pl.semaphore_signal(barrier, inc=1, device_id={"dom": peer}, device_id_type=DEVICE_MESH)
    for peer in feat_peers:
        pl.semaphore_signal(barrier, inc=1, device_id={"feat": peer}, device_id_type=DEVICE_MESH)
    pl.semaphore_signal(barrier, inc=1, device_id=sibling, device_id_type=DEVICE_MESH)
    pl.semaphore_wait(barrier, n_dom + n_feat - 1)

    got_latent.wait()
    first_latents = [
        send(latents.at[0, feat, own_rows, :], latents.at[0, feat, own_rows, :], {"feat": peer})
        for peer in feat_peers
    ]

    got_grid.wait()
    got_sender.wait()

    def band_rows(source):
        return pl.ds(source * (2 * half_units) + sub * half_units, half_units)

    def project(peer):
        values = jnp.dot(grid_half[peer], sender_w[0], preferred_element_type=F32)
        return values.astype(BF16).reshape(half_units, half_tile, width)

    steps = sorted(range(1, n_dom), key=lambda step: -min(step, n_dom - step))
    grid_copies = []
    for step in steps:
        peer = lax.rem(dom + step, n_dom)
        grid_out[step - 1] = project(peer)
        grid_copies.append(
            send(grid_out.at[step - 1], grid_table.at[band_rows(dom)], {"dom": peer})
        )
    grid_table[band_rows(dom)] = project(dom)
    share_grid = [
        send(grid_table.at[band_rows(dom)], grid_table.at[band_rows(dom)], sibling)
    ]

    got_output.wait()
    got_gain.wait()
    model_half = pl.ds(pl.multiple_of(sub * half_model, half_model), half_model)
    weight_copies = []
    for layer in range(LAYERS):
        part = output_w.at[feat, layer, model_half, :]
        weight_copies.append([send(part, part, {"feat": peer}) for peer in feat_peers])
    gain_copies = [send(gain.at[feat], gain.at[feat], {"feat": peer}) for peer in feat_peers]

    def geometry_terms(geometry, layer, target):
        def body(pair, carry):
            rows = pl.ds(pl.multiple_of(pair * 2 * TILE, 2 * TILE), 2 * TILE)
            target[rows, :] = (
                contract_rows(geometry[:, rows], edge_weight[layer], lax.Precision.HIGHEST)
                + edge_bias[pl.ds(layer, 1), :]
            )
            return carry

        lax.fori_loop(0, target.shape[0] // (2 * TILE), body, 0)

    geometry_terms(encoder_geometry, 0, terms_enc)

    share_first = []
    for source, copy in zip(feat_sources, first_latents):
        copy.wait_recv()
        part = latents.at[0, source, own_rows, :]
        share_first.append(send(part, part, sibling))

    for layer in range(1, LAYERS):
        geometry_terms(mesh_geometry, layer, terms_mesh.at[layer - 1])

    got_receiver.wait()
    got_node.wait()
    for copy in share_first:
        copy.wait_recv()

    def whole(layer, rows):
        return jnp.concatenate([latents[layer, f, rows, :] for f in range(n_feat)], axis=1)

    def widen(layer):
        base[0] = jnp.dot(whole(layer, own_rows), node_w[layer], preferred_element_type=F32)
        receivers[...] = jnp.dot(
            whole(layer, slice(None)), receiver_w[layer], preferred_element_type=F32
        ).reshape(receivers.shape)

    widen(0)

    for step, copy in zip(steps, grid_copies):
        copy.wait_recv()
        source = lax.rem(dom + n_dom - step, n_dom)
        part = grid_table.at[band_rows(source)]
        share_grid.append(send(part, part, sibling))
    for copy in share_grid:
        copy.wait_recv()

    def edge_sums(lanes, terms, load, row):
        blocks = 2 * lanes.shape[0]
        zero_slot = blocks
        sums[zero_slot] = jnp.zeros((TILE, width), F32)
        lane_at = lax.broadcasted_iota(jnp.int32, (1, 2 * TILE), 1)
        shift = jnp.where(lane_at >= TILE, TILE, 0)
        row_at = lax.broadcasted_iota(jnp.int32, (2 * TILE, 2 * TILE), 0)

        def body(pair, carry):
            rows = pl.ds(pl.multiple_of(pair * 2 * TILE, 2 * TILE), 2 * TILE)
            wanted = lanes[pl.ds(pair, 1), :] + shift
            chosen = jnp.where(row_at == wanted, 1.0, 0.0).astype(BF16)
            source = jnp.concatenate(
                [load(plan[row, 2 * pair]), load(plan[row, 2 * pair + 1])], axis=0
            )
            before = contract_rows(chosen, source) + terms[rows, :]
            for side in range(2):
                block = 2 * pair + side
                message = silu(
                    before[side * TILE : (side + 1) * TILE] + receivers[plan[row + 3, block]]
                )
                sums[block] = message + sums[plan[row + 1, block]]
            return carry

        lax.fori_loop(0, blocks // 2, body, 0)

    def load_grid(tile):
        return jnp.concatenate([grid_table[2 * tile], grid_table[2 * tile + 1]], axis=0)

    for layer in range(LAYERS):
        if layer == 0:
            edge_sums(encoder_lanes, terms_enc, load_grid, 0)
        else:
            senders = (
                jnp.dot(whole(layer, slice(None)), sender_w[layer], preferred_element_type=F32)
                .astype(BF16)
                .reshape(tile_count, TILE, width)
            )
            local_table[...] = senders
            tables[layer - 1][:tile_count] = senders
            table = tables[layer - 1]
            half = pl.ds(pl.multiple_of(sub * half_tile, half_tile), half_tile)
            halo_copies = []
            for way, step in enumerate((1, n_dom - 1, n_dom // 2)):
                peer = lax.rem(dom + step, n_dom)
                for slot in range(CAP):
                    listed = local_table[plan[8, CAP * way + slot]]
                    halo_out[layer - 1, way, slot] = jnp.where(
                        sub == 0, listed[:half_tile], listed[half_tile:]
                    )
                halo_copies.append(
                    send(
                        halo_out.at[layer - 1, way],
                        table.at[pl.ds(tile_count + CAP * way, CAP), half, :],
                        {"dom": peer},
                    )
                )
            widen(layer)
            share_halo = []
            for way, copy in enumerate(halo_copies):
                copy.wait_recv()
                part = table.at[pl.ds(tile_count + CAP * way, CAP), half, :]
                share_halo.append(send(part, part, sibling))
            for copy in share_halo:
                copy.wait_recv()
            edge_sums(mesh_lanes, terms_mesh.at[layer - 1], lambda at: table[at], 4)

        ends = 2 if layer == 0 else 6
        for k in range(half_tiles):
            theirs = plan[ends, (1 - sub) * half_tiles + k]
            share_out[layer, k] = sums[theirs]
        sum_copy = send(share_out.at[layer], share_in.at[layer], sibling)
        for k in range(half_tiles):
            mine = plan[ends, sub * half_tiles + k]
            rows = slice(k * TILE, (k + 1) * TILE)
            base[0, rows, :] = base[0, rows, :] + sums[mine]
        if layer == 0:
            share_weights = []
            for at in range(LAYERS):
                share_weights.append([])
                for source, copy in zip(feat_sources, weight_copies[at]):
                    copy.wait_recv()
                    part = output_w.at[source, at, model_half, :]
                    share_weights[at].append(send(part, part, sibling))
            for copy in gain_copies:
                copy.wait_recv()
        sum_copy.wait_recv()
        active = silu(
            base[0]
            + share_in[layer].reshape(half_rows, width)
            + node_bias[pl.ds(layer, 1), :]
        ).astype(BF16)
        for f in range(n_feat):
            hidden[layer, 0, f] = active[f * part_rows : (f + 1) * part_rows]
        hidden_copies = [
            send(hidden.at[layer, 0, peer], hidden.at[layer, 1, feat], {"feat": peer})
            for peer in feat_peers
        ]
        hidden[layer, 1, feat] = hidden[layer, 0, feat]
        for copy in hidden_copies:
            copy.wait_recv()
        for copy in share_weights[layer]:
            copy.wait_recv()
        whole_hidden = jnp.concatenate([hidden[layer, 1, f] for f in range(n_feat)], axis=1)
        updates = [
            jnp.dot(whole_hidden, output_w[f, layer], preferred_element_type=F32)
            for f in range(n_feat)
        ]
        row_mean = sum(jnp.sum(u, axis=1, keepdims=True) for u in updates) / model_width
        row_squares = sum(jnp.sum(u * u, axis=1, keepdims=True) for u in updates) / model_width
        scale = lax.rsqrt(row_squares - row_mean * row_mean + EPSILON)
        def part_of(source):
            return pl.ds(
                pl.multiple_of(sub * half_rows + source * part_rows, part_rows), part_rows
            )

        mine = part_of(feat)
        for f in range(n_feat):
            normed = (updates[f] - row_mean) * scale * gain[f, pl.ds(layer, 1), :]
            latents[layer + 1, f, mine, :] = (
                latents[layer, f, mine, :].astype(F32) + normed
            ).astype(BF16)
        columns = (lambda device: pl.ds(0, n_feat)) if layer < LAYERS - 1 else (lambda device: device)
        latent_copies = [
            send(
                latents.at[layer + 1, columns(peer), mine, :],
                latents.at[layer + 1, columns(peer), mine, :],
                {"feat": peer},
            )
            for peer in feat_peers
        ]
        part = latents.at[layer + 1, columns(feat), mine, :]
        share_latent = [send(part, part, sibling)]
        for source, copy in zip(feat_sources, latent_copies):
            copy.wait_recv()
            part = latents.at[layer + 1, columns(feat), part_of(source), :]
            share_latent.append(send(part, part, sibling))
        for copy in share_latent:
            copy.wait_recv()

    out[...] = latents[LAYERS, feat]
    for copy in sends:
        copy.wait_send()


def local(
    n_dom,
    n_feat,
    grid_latent,
    mesh_latent,
    encoder_tiles,
    encoder_lanes,
    encoder_geometry,
    halo_tiles,
    mesh_tiles,
    mesh_lanes,
    mesh_geometry,
    sender_weight,
    receiver_weight,
    node_weight,
    edge_weight,
    edge_bias,
    node_bias,
    output_weight,
    norm_gain,
):
    model, width = sender_weight.shape[1:]
    grid_rows = grid_latent.shape[0]
    mesh_rows = mesh_latent.shape[0]
    tile_count = mesh_rows // TILE
    band = grid_rows // n_dom
    enc_edges = encoder_lanes.shape[0]
    mesh_edges = mesh_lanes.shape[0]
    half_rows = mesh_rows // 2
    part_rows = half_rows // n_feat
    copies = 2 * n_dom + 16 + (n_feat - 1) * (2 + 2 * LAYERS + 1 + 3 * LAYERS) + 2 * LAYERS
    copies += 6 * (LAYERS - 1)
    smem = pl.BlockSpec(memory_space=pltpu.SMEM)
    plan = pl.pallas_call(
        functools.partial(plan_kernel, n_dom, tile_count),
        out_shape=jax.ShapeDtypeStruct((9, max(enc_edges, mesh_edges) // TILE), jnp.int32),
        in_specs=[smem] * 3,
        out_specs=smem,
        scratch_shapes=[pltpu.SMEM((tile_count,), jnp.int32)],
    )(encoder_tiles, mesh_tiles, halo_tiles)
    vmem = pl.BlockSpec(memory_space=pltpu.VMEM)
    far = pl.BlockSpec(memory_space=pl.ANY)
    return pl.pallas_call(
        functools.partial(kernel, (n_dom, n_feat)),
        out_shape=jax.ShapeDtypeStruct((mesh_rows, width), BF16),
        in_specs=[smem] + [vmem] * 7 + [far] * 7,
        out_specs=vmem,
        scratch_shapes=[
            pltpu.VMEM((n_dom, band // 2, model), BF16),
            pltpu.VMEM((LAYERS, model, width), BF16),
            pltpu.VMEM((LAYERS, model, width), BF16),
            pltpu.VMEM((LAYERS, model, width), BF16),
            pltpu.VMEM((n_feat, LAYERS, model, width), BF16),
            pltpu.VMEM((n_feat, LAYERS, width), F32),
            pltpu.VMEM((n_dom - 1, band // TILE, TILE // 2, width), BF16),
            pltpu.VMEM((2 * grid_rows // TILE, TILE // 2, width), BF16),
            pltpu.VMEM((LAYERS + 1, n_feat, mesh_rows, width), BF16),
            pltpu.VMEM((tile_count + 3 * CAP, TILE, width), BF16),
            pltpu.VMEM((tile_count + 3 * CAP, TILE, width), BF16),
            pltpu.VMEM((tile_count, TILE, width), BF16),
            pltpu.VMEM((LAYERS - 1, 3, CAP, TILE // 2, width), BF16),
            pltpu.VMEM((tile_count, TILE, width), F32),
            pltpu.VMEM((1, half_rows, width), F32),
            pltpu.VMEM((enc_edges, width), F32),
            pltpu.VMEM((LAYERS - 1, mesh_edges, width), F32),
            pltpu.VMEM((max(enc_edges, mesh_edges) // TILE + 1, TILE, width), F32),
            pltpu.VMEM((LAYERS, tile_count // 2, TILE, width), F32),
            pltpu.VMEM((LAYERS, tile_count // 2, TILE, width), F32),
            pltpu.VMEM((LAYERS, 2, n_feat, part_rows, width), BF16),
            pltpu.SemaphoreType.DMA((8,)),
            pltpu.SemaphoreType.DMA((copies,)),
            pltpu.SemaphoreType.DMA((copies,)),
        ],
        compiler_params=pltpu.CompilerParams(
            collective_id=0, has_side_effects=True, vmem_limit_bytes=48 * 1024 * 1024
        ),
    )(
        plan,
        encoder_lanes.reshape(-1, 2 * TILE),
        mesh_lanes.reshape(-1, 2 * TILE),
        encoder_geometry,
        mesh_geometry,
        edge_weight,
        edge_bias,
        node_bias,
        grid_latent.reshape(n_dom, band, model),
        mesh_latent,
        sender_weight,
        receiver_weight,
        node_weight,
        output_weight,
        norm_gain,
    )


def solution(mesh):
    in_specs = (
        P(("groups", "dom"), None),
        P(("groups", "dom"), "feat"),
        P(None, ("dom", "sub")),
        P(("dom", "sub")),
        P(None, ("dom", "sub")),
        P("dom", None, None),
        P(None, ("dom", "sub")),
        P(("dom", "sub")),
        P(None, ("dom", "sub")),
        P(None, None, "feat"),
        P(None, None, "feat"),
        P(None, None, "feat"),
        P(None, None, "feat"),
        P(None, "feat"),
        P(None, "feat"),
        P(None, None, "feat"),
        P(None, "feat"),
    )
    out_specs = P(("groups", "dom"), "feat")
    return jax.shard_map(
        functools.partial(local, mesh.shape["dom"], mesh.shape["feat"]),
        mesh=mesh,
        in_specs=in_specs,
        out_specs=out_specs,
        check_vma=False,
    )
```

```python
import functools

import jax
import jax.numpy as jnp
from jax import lax
from jax.experimental import pallas as pl
from jax.experimental.pallas import tpu as pltpu
from jax.sharding import PartitionSpec as P

TILE = 64
LAYERS = 3
CAP = 3
EPSILON = 1e-05
VMEM_GRANT = 63 * 1024 * 1024
DEVICE_MESH = pl.DeviceIdType.MESH
F32 = jnp.float32
BF16 = jnp.bfloat16


def silu(value):
    half = 0.5 * value
    return half + half * jnp.tanh(half)


def contract_rows(left, right, precision=None):
    return lax.dot_general(
        left, right, (((0,), (0,)), ((), ())), preferred_element_type=F32, precision=precision
    )


def plan_kernel(n_dom, tile_count, encoder_tiles, mesh_tiles, halo_tiles, plan, last):
    dom = lax.axis_index("dom")
    previous = lax.rem(dom + n_dom - 1, n_dom)
    following = lax.rem(dom + 1, n_dom)

    def chain(tiles, row):
        blocks = tiles.shape[1]

        def clear(t, carry):
            last[t] = blocks
            return carry

        def follow(block, carry):
            target = tiles[1, block]
            plan[row + 1, block] = last[target]
            plan[row + 3, block] = target
            last[target] = block
            return carry

        def keep(t, carry):
            plan[row + 2, t] = last[t]
            return carry

        lax.fori_loop(0, tile_count, clear, 0)
        lax.fori_loop(0, blocks, follow, 0)
        lax.fori_loop(0, tile_count, keep, 0)

    def grid_place(block, carry):
        plan[0, block] = encoder_tiles[0, block]
        return carry

    def mesh_place(block, carry):
        tile = mesh_tiles[0, block]
        beyond = jnp.maximum(tile - tile_count, 0)
        owner = lax.div(beyond, CAP)
        slot = lax.rem(beyond, CAP)
        way = jnp.where(owner == previous, 0, jnp.where(owner == following, 1, 2))
        plan[4, block] = jnp.where(tile < tile_count, tile, tile_count + CAP * way + slot)
        return carry

    lax.fori_loop(0, encoder_tiles.shape[1], grid_place, 0)
    lax.fori_loop(0, mesh_tiles.shape[1], mesh_place, 0)
    chain(encoder_tiles, 0)
    chain(mesh_tiles, 4)
    for way, step in enumerate((1, n_dom - 1, n_dom // 2)):
        peer = lax.rem(dom + step, n_dom)
        for slot in range(CAP):
            plan[8, CAP * way + slot] = jnp.maximum(halo_tiles[0, peer, slot], 0)


def kernel(
    sizes,
    plan,
    far_encoder_lanes,
    far_mesh_lanes,
    far_encoder_geometry,
    far_mesh_geometry,
    far_edge_weight,
    far_edge_bias,
    far_node_bias,
    grid_latent,
    mesh_latent,
    sender_weight,
    receiver_weight,
    node_weight,
    output_weight,
    norm_gain,
    out,
    encoder_lanes,
    mesh_lanes,
    encoder_geometry,
    mesh_geometry,
    edge_weight,
    edge_bias,
    node_bias,
    grid_half,
    sender_w,
    receiver_w,
    node_w,
    output_w,
    gain,
    grid_out,
    grid_table,
    latents,
    first_table,
    second_table,
    local_table,
    halo_out,
    receivers,
    base,
    terms_enc,
    terms_mesh,
    sums,
    share_out,
    share_in,
    hidden,
    fetch_sem,
    send_sem,
    recv_sem,
):
    n_dom, n_feat = sizes
    dom = lax.axis_index("dom")
    feat = lax.axis_index("feat")
    sub = lax.axis_index("sub")
    width = base.shape[2]
    mesh_rows = latents.shape[2]
    tile_count = mesh_rows // TILE
    half_tiles = tile_count // 2
    half_rows = mesh_rows // 2
    part_rows = half_rows // n_feat
    half_band = grid_half.shape[1]
    model_width = grid_half.shape[2]
    half_model = model_width // 2
    half_tile = TILE // 2
    half_units = half_band // half_tile

    tables = (first_table, second_table)
    fetches = []
    sends = []

    def fetch(source, target):
        copy = pltpu.make_async_copy(source, target, fetch_sem.at[len(fetches)])
        copy.start()
        fetches.append(copy)
        return copy

    def send(source, target, device):
        slot = len(sends)
        copy = pltpu.make_async_remote_copy(
            src_ref=source,
            dst_ref=target,
            send_sem=send_sem.at[slot],
            recv_sem=recv_sem.at[slot],
            device_id=device,
            device_id_type=DEVICE_MESH,
        )
        copy.start()
        sends.append(copy)
        return copy

    sibling = {"sub": 1 - sub}
    own_rows = pl.ds(pl.multiple_of(sub * half_rows, half_rows), half_rows)

    got_grid = fetch(
        grid_latent.at[:, pl.ds(pl.multiple_of(sub * half_band, half_band), half_band), :], grid_half
    )
    got_sender = fetch(sender_weight, sender_w)
    got_latent = fetch(mesh_latent, latents.at[0, feat])
    got_receiver = fetch(receiver_weight, receiver_w)
    got_node = fetch(node_weight, node_w)
    got_output = fetch(output_weight, output_w.at[feat])
    got_gain = fetch(norm_gain, gain.at[feat])
    got_rest = [
        fetch(far_encoder_geometry, encoder_geometry),
        fetch(far_edge_weight, edge_weight),
        fetch(far_edge_bias, edge_bias),
        fetch(far_mesh_geometry, mesh_geometry),
        fetch(far_encoder_lanes, encoder_lanes),
        fetch(far_mesh_lanes, mesh_lanes),
        fetch(far_node_bias, node_bias),
    ]

    barrier = pltpu.get_barrier_semaphore()
    dom_peers = [lax.rem(dom + step, n_dom) for step in range(1, n_dom)]
    feat_peers = [lax.rem(feat + step, n_feat) for step in range(1, n_feat)]
    feat_sources = [lax.rem(feat + n_feat - step, n_feat) for step in range(1, n_feat)]
    for peer in dom_peers:
        pl.semaphore_signal(barrier, inc=1, device_id={"dom": peer}, device_id_type=DEVICE_MESH)
    for peer in feat_peers:
        pl.semaphore_signal(barrier, inc=1, device_id={"feat": peer}, device_id_type=DEVICE_MESH)
    pl.semaphore_signal(barrier, inc=1, device_id=sibling, device_id_type=DEVICE_MESH)
    pl.semaphore_wait(barrier, n_dom + n_feat - 1)

    got_latent.wait()
    first_latents = [
        send(latents.at[0, feat, own_rows, :], latents.at[0, feat, own_rows, :], {"feat": peer})
        for peer in feat_peers
    ]

    got_grid.wait()
    got_sender.wait()

    def band_rows(source):
        return pl.ds(source * (2 * half_units) + sub * half_units, half_units)

    def project(peer):
        values = jnp.dot(grid_half[peer], sender_w[0], preferred_element_type=F32)
        return values.astype(BF16).reshape(half_units, half_tile, width)

    steps = sorted(range(1, n_dom), key=lambda step: -min(step, n_dom - step))
    grid_copies = []
    for step in steps:
        peer = lax.rem(dom + step, n_dom)
        grid_out[step - 1] = project(peer)
        grid_copies.append(
            send(grid_out.at[step - 1], grid_table.at[band_rows(dom)], {"dom": peer})
        )
    grid_table[band_rows(dom)] = project(dom)
    share_grid = [
        send(grid_table.at[band_rows(dom)], grid_table.at[band_rows(dom)], sibling)
    ]

    got_output.wait()
    got_gain.wait()
    model_half = pl.ds(pl.multiple_of(sub * half_model, half_model), half_model)
    weight_copies = []
    for layer in range(LAYERS):
        part = output_w.at[feat, layer, model_half, :]
        weight_copies.append([send(part, part, {"feat": peer}) for peer in feat_peers])
    gain_copies = [send(gain.at[feat], gain.at[feat], {"feat": peer}) for peer in feat_peers]

    def geometry_terms(geometry, layer, target):
        def body(pair, carry):
            rows = pl.ds(pl.multiple_of(pair * 2 * TILE, 2 * TILE), 2 * TILE)
            target[rows, :] = (
                contract_rows(geometry[:, rows], edge_weight[layer], lax.Precision.HIGHEST)
                + edge_bias[pl.ds(layer, 1), :]
            )
            return carry

        lax.fori_loop(0, target.shape[0] // (2 * TILE), body, 0)

    for copy in got_rest:
        copy.wait()
    geometry_terms(encoder_geometry, 0, terms_enc)

    share_first = []
    for source, copy in zip(feat_sources, first_latents):
        copy.wait_recv()
        part = latents.at[0, source, own_rows, :]
        share_first.append(send(part, part, sibling))

    for layer in range(1, LAYERS):
        geometry_terms(mesh_geometry, layer, terms_mesh.at[layer - 1])

    got_receiver.wait()
    got_node.wait()
    for copy in share_first:
        copy.wait_recv()

    def whole(layer, rows):
        return jnp.concatenate([latents[layer, f, rows, :] for f in range(n_feat)], axis=1)

    def widen(layer):
        base[0] = jnp.dot(whole(layer, own_rows), node_w[layer], preferred_element_type=F32)
        receivers[...] = jnp.dot(
            whole(layer, slice(None)), receiver_w[layer], preferred_element_type=F32
        ).reshape(receivers.shape)

    widen(0)

    for step, copy in zip(steps, grid_copies):
        copy.wait_recv()
        source = lax.rem(dom + n_dom - step, n_dom)
        part = grid_table.at[band_rows(source)]
        share_grid.append(send(part, part, sibling))
    for copy in share_grid:
        copy.wait_recv()

    def edge_sums(lanes, terms, load, row):
        blocks = 2 * lanes.shape[0]
        zero_slot = blocks
        sums[zero_slot] = jnp.zeros((TILE, width), F32)
        lane_at = lax.broadcasted_iota(jnp.int32, (1, 2 * TILE), 1)
        shift = jnp.where(lane_at >= TILE, TILE, 0)
        row_at = lax.broadcasted_iota(jnp.int32, (2 * TILE, 2 * TILE), 0)

        def body(pair, carry):
            rows = pl.ds(pl.multiple_of(pair * 2 * TILE, 2 * TILE), 2 * TILE)
            wanted = lanes[pl.ds(pair, 1), :] + shift
            chosen = jnp.where(row_at == wanted, 1.0, 0.0).astype(BF16)
            source = jnp.concatenate(
                [load(plan[row, 2 * pair]), load(plan[row, 2 * pair + 1])], axis=0
            )
            before = contract_rows(chosen, source) + terms[rows, :]
            for side in range(2):
                block = 2 * pair + side
                message = silu(
                    before[side * TILE : (side + 1) * TILE] + receivers[plan[row + 3, block]]
                )
                sums[block] = message + sums[plan[row + 1, block]]
            return carry

        lax.fori_loop(0, blocks // 2, body, 0)

    def load_grid(tile):
        return jnp.concatenate([grid_table[2 * tile], grid_table[2 * tile + 1]], axis=0)

    for layer in range(LAYERS):
        if layer == 0:
            edge_sums(encoder_lanes, terms_enc, load_grid, 0)
        else:
            senders = (
                jnp.dot(whole(layer, slice(None)), sender_w[layer], preferred_element_type=F32)
                .astype(BF16)
                .reshape(tile_count, TILE, width)
            )
            local_table[...] = senders
            tables[layer - 1][:tile_count] = senders
            table = tables[layer - 1]
            half = pl.ds(pl.multiple_of(sub * half_tile, half_tile), half_tile)
            halo_copies = []
            for way, step in enumerate((1, n_dom - 1, n_dom // 2)):
                peer = lax.rem(dom + step, n_dom)
                for slot in range(CAP):
                    listed = local_table[plan[8, CAP * way + slot]]
                    halo_out[layer - 1, way, slot] = jnp.where(
                        sub == 0, listed[:half_tile], listed[half_tile:]
                    )
                halo_copies.append(
                    send(
                        halo_out.at[layer - 1, way],
                        table.at[pl.ds(tile_count + CAP * way, CAP), half, :],
                        {"dom": peer},
                    )
                )
            widen(layer)
            share_halo = []
            for way, copy in enumerate(halo_copies):
                copy.wait_recv()
                part = table.at[pl.ds(tile_count + CAP * way, CAP), half, :]
                share_halo.append(send(part, part, sibling))
            for copy in share_halo:
                copy.wait_recv()
            edge_sums(mesh_lanes, terms_mesh.at[layer - 1], lambda at: table[at], 4)

        ends = 2 if layer == 0 else 6
        for k in range(half_tiles):
            theirs = plan[ends, (1 - sub) * half_tiles + k]
            share_out[layer, k] = sums[theirs]
        sum_copy = send(share_out.at[layer], share_in.at[layer], sibling)
        for k in range(half_tiles):
            mine = plan[ends, sub * half_tiles + k]
            rows = slice(k * TILE, (k + 1) * TILE)
            base[0, rows, :] = base[0, rows, :] + sums[mine]
        if layer == 0:
            share_weights = []
            for at in range(LAYERS):
                share_weights.append([])
                for source, copy in zip(feat_sources, weight_copies[at]):
                    copy.wait_recv()
                    part = output_w.at[source, at, model_half, :]
                    share_weights[at].append(send(part, part, sibling))
            for copy in gain_copies:
                copy.wait_recv()
        sum_copy.wait_recv()
        active = silu(
            base[0]
            + share_in[layer].reshape(half_rows, width)
            + node_bias[pl.ds(layer, 1), :]
        ).astype(BF16)
        for f in range(n_feat):
            hidden[layer, 0, f] = active[f * part_rows : (f + 1) * part_rows]
        hidden_copies = [
            send(hidden.at[layer, 0, peer], hidden.at[layer, 1, feat], {"feat": peer})
            for peer in feat_peers
        ]
        hidden[layer, 1, feat] = hidden[layer, 0, feat]
        for copy in hidden_copies:
            copy.wait_recv()
        for copy in share_weights[layer]:
            copy.wait_recv()
        whole_hidden = jnp.concatenate([hidden[layer, 1, f] for f in range(n_feat)], axis=1)
        updates = [
            jnp.dot(whole_hidden, output_w[f, layer], preferred_element_type=F32)
            for f in range(n_feat)
        ]
        row_mean = sum(jnp.sum(u, axis=1, keepdims=True) for u in updates) / model_width
        row_squares = sum(jnp.sum(u * u, axis=1, keepdims=True) for u in updates) / model_width
        scale = lax.rsqrt(row_squares - row_mean * row_mean + EPSILON)
        def part_of(source):
            return pl.ds(
                pl.multiple_of(sub * half_rows + source * part_rows, part_rows), part_rows
            )

        mine = part_of(feat)
        for f in range(n_feat):
            normed = (updates[f] - row_mean) * scale * gain[f, pl.ds(layer, 1), :]
            latents[layer + 1, f, mine, :] = (
                latents[layer, f, mine, :].astype(F32) + normed
            ).astype(BF16)
        columns = (lambda device: pl.ds(0, n_feat)) if layer < LAYERS - 1 else (lambda device: device)
        latent_copies = [
            send(
                latents.at[layer + 1, columns(peer), mine, :],
                latents.at[layer + 1, columns(peer), mine, :],
                {"feat": peer},
            )
            for peer in feat_peers
        ]
        part = latents.at[layer + 1, columns(feat), mine, :]
        share_latent = [send(part, part, sibling)]
        for source, copy in zip(feat_sources, latent_copies):
            copy.wait_recv()
            part = latents.at[layer + 1, columns(feat), part_of(source), :]
            share_latent.append(send(part, part, sibling))
        for copy in share_latent:
            copy.wait_recv()

    out[...] = latents[LAYERS, feat]
    for copy in sends:
        copy.wait_send()


def local(
    n_dom,
    n_feat,
    grid_latent,
    mesh_latent,
    encoder_tiles,
    encoder_lanes,
    encoder_geometry,
    halo_tiles,
    mesh_tiles,
    mesh_lanes,
    mesh_geometry,
    sender_weight,
    receiver_weight,
    node_weight,
    edge_weight,
    edge_bias,
    node_bias,
    output_weight,
    norm_gain,
):
    model, width = sender_weight.shape[1:]
    grid_rows = grid_latent.shape[0]
    mesh_rows = mesh_latent.shape[0]
    tile_count = mesh_rows // TILE
    band = grid_rows // n_dom
    enc_edges = encoder_lanes.shape[0]
    mesh_edges = mesh_lanes.shape[0]
    half_rows = mesh_rows // 2
    part_rows = half_rows // n_feat
    copies = 2 * n_dom + 16 + (n_feat - 1) * (2 + 2 * LAYERS + 1 + 3 * LAYERS) + 2 * LAYERS
    copies += 6 * (LAYERS - 1)
    smem = pl.BlockSpec(memory_space=pltpu.SMEM)
    plan = pl.pallas_call(
        functools.partial(plan_kernel, n_dom, tile_count),
        out_shape=jax.ShapeDtypeStruct((9, max(enc_edges, mesh_edges) // TILE), jnp.int32),
        in_specs=[smem] * 3,
        out_specs=smem,
        scratch_shapes=[pltpu.SMEM((tile_count,), jnp.int32)],
        compiler_params=pltpu.CompilerParams(vmem_limit_bytes=VMEM_GRANT),
    )(encoder_tiles, mesh_tiles, halo_tiles)
    vmem = pl.BlockSpec(memory_space=pltpu.VMEM)
    far = pl.BlockSpec(memory_space=pltpu.HBM)
    return pl.pallas_call(
        functools.partial(kernel, (n_dom, n_feat)),
        out_shape=jax.ShapeDtypeStruct((mesh_rows, width), BF16),
        in_specs=[smem] + [far] * 14,
        out_specs=vmem,
        scratch_shapes=[
            pltpu.VMEM((enc_edges // (2 * TILE), 2 * TILE), jnp.int32),
            pltpu.VMEM((mesh_edges // (2 * TILE), 2 * TILE), jnp.int32),
            pltpu.VMEM(encoder_geometry.shape, F32),
            pltpu.VMEM(mesh_geometry.shape, F32),
            pltpu.VMEM(edge_weight.shape, F32),
            pltpu.VMEM(edge_bias.shape, F32),
            pltpu.VMEM(node_bias.shape, F32),
            pltpu.VMEM((n_dom, band // 2, model), BF16),
            pltpu.VMEM((LAYERS, model, width), BF16),
            pltpu.VMEM((LAYERS, model, width), BF16),
            pltpu.VMEM((LAYERS, model, width), BF16),
            pltpu.VMEM((n_feat, LAYERS, model, width), BF16),
            pltpu.VMEM((n_feat, LAYERS, width), F32),
            pltpu.VMEM((n_dom - 1, band // TILE, TILE // 2, width), BF16),
            pltpu.VMEM((2 * grid_rows // TILE, TILE // 2, width), BF16),
            pltpu.VMEM((LAYERS + 1, n_feat, mesh_rows, width), BF16),
            pltpu.VMEM((tile_count + 3 * CAP, TILE, width), BF16),
            pltpu.VMEM((tile_count + 3 * CAP, TILE, width), BF16),
            pltpu.VMEM((tile_count, TILE, width), BF16),
            pltpu.VMEM((LAYERS - 1, 3, CAP, TILE // 2, width), BF16),
            pltpu.VMEM((tile_count, TILE, width), F32),
            pltpu.VMEM((1, half_rows, width), F32),
            pltpu.VMEM((enc_edges, width), F32),
            pltpu.VMEM((LAYERS - 1, mesh_edges, width), F32),
            pltpu.VMEM((max(enc_edges, mesh_edges) // TILE + 1, TILE, width), F32),
            pltpu.VMEM((LAYERS, tile_count // 2, TILE, width), F32),
            pltpu.VMEM((LAYERS, tile_count // 2, TILE, width), F32),
            pltpu.VMEM((LAYERS, 2, n_feat, part_rows, width), BF16),
            pltpu.SemaphoreType.DMA((14,)),
            pltpu.SemaphoreType.DMA((copies,)),
            pltpu.SemaphoreType.DMA((copies,)),
        ],
        compiler_params=pltpu.CompilerParams(
            collective_id=0, has_side_effects=True, vmem_limit_bytes=VMEM_GRANT
        ),
    )(
        plan,
        encoder_lanes.reshape(-1, 2 * TILE),
        mesh_lanes.reshape(-1, 2 * TILE),
        encoder_geometry,
        mesh_geometry,
        edge_weight,
        edge_bias,
        node_bias,
        grid_latent.reshape(n_dom, band, model),
        mesh_latent,
        sender_weight,
        receiver_weight,
        node_weight,
        output_weight,
        norm_gain,
    )


def solution(mesh):
    in_specs = (
        P(("groups", "dom"), None),
        P(("groups", "dom"), "feat"),
        P(None, ("dom", "sub")),
        P(("dom", "sub")),
        P(None, ("dom", "sub")),
        P("dom", None, None),
        P(None, ("dom", "sub")),
        P(("dom", "sub")),
        P(None, ("dom", "sub")),
        P(None, None, "feat"),
        P(None, None, "feat"),
        P(None, None, "feat"),
        P(None, None, "feat"),
        P(None, "feat"),
        P(None, "feat"),
        P(None, None, "feat"),
        P(None, "feat"),
    )
    out_specs = P(("groups", "dom"), "feat")
    return jax.shard_map(
        functools.partial(local, mesh.shape["dom"], mesh.shape["feat"]),
        mesh=mesh,
        in_specs=in_specs,
        out_specs=out_specs,
        check_vma=False,
    )
```

```python
import functools

import jax
import jax.numpy as jnp
from jax import lax
from jax.experimental import pallas as pl
from jax.experimental.pallas import tpu as pltpu
from jax.sharding import PartitionSpec as P

TILE = 64
LAYERS = 3
CAP = 3
CHUNK = 2
SPLIT_ROWS = 32
EPSILON = 1e-05
VMEM_GRANT = 63 * 1024 * 1024
DEVICE_MESH = pl.DeviceIdType.MESH
F32 = jnp.float32
BF16 = jnp.bfloat16


def silu(value):
    half = 0.5 * value
    return half + half * jnp.tanh(half)


def contract_rows(left, right):
    return lax.dot_general(
        left, right, (((0,), (0,)), ((), ())), preferred_element_type=F32
    )


def plan_kernel(n_dom, tile_count, encoder_tiles, mesh_tiles, halo_tiles, plan, last):
    dom = lax.axis_index("dom")
    previous = lax.rem(dom + n_dom - 1, n_dom)
    following = lax.rem(dom + 1, n_dom)

    def chain(tiles, row):
        blocks = tiles.shape[1]

        def clear(t, carry):
            last[t] = blocks
            return carry

        def follow(block, carry):
            target = tiles[1, block]
            plan[row + 1, block] = last[target]
            plan[row + 3, block] = target
            last[target] = block
            return carry

        def keep(t, carry):
            plan[row + 2, t] = last[t]
            return carry

        lax.fori_loop(0, tile_count, clear, 0)
        lax.fori_loop(0, blocks, follow, 0)
        lax.fori_loop(0, tile_count, keep, 0)

    def grid_place(block, carry):
        plan[0, block] = encoder_tiles[0, block]
        return carry

    def mesh_place(block, carry):
        tile = mesh_tiles[0, block]
        beyond = jnp.maximum(tile - tile_count, 0)
        owner = lax.div(beyond, CAP)
        slot = lax.rem(beyond, CAP)
        way = jnp.where(owner == previous, 0, jnp.where(owner == following, 1, 2))
        plan[4, block] = jnp.where(tile < tile_count, tile, tile_count + CAP * way + slot)
        return carry

    lax.fori_loop(0, encoder_tiles.shape[1], grid_place, 0)
    lax.fori_loop(0, mesh_tiles.shape[1], mesh_place, 0)
    chain(encoder_tiles, 0)
    chain(mesh_tiles, 4)
    for way, step in enumerate((1, n_dom - 1, n_dom // 2)):
        peer = lax.rem(dom + step, n_dom)
        for slot in range(CAP):
            plan[8, CAP * way + slot] = jnp.maximum(halo_tiles[slot, 0, peer], 0)


def kernel(
    sizes,
    plan,
    far_encoder_lanes,
    far_mesh_lanes,
    far_encoder_geometry,
    far_mesh_geometry,
    far_edge_weight,
    far_edge_bias,
    far_node_bias,
    grid_latent,
    mesh_latent,
    sender_weight,
    receiver_weight,
    node_weight,
    output_weight,
    norm_gain,
    out,
    encoder_lanes,
    mesh_lanes,
    encoder_geometry,
    mesh_geometry,
    edge_weight,
    edge_bias,
    node_bias,
    grid_half,
    sender_w,
    receiver_w,
    node_w,
    output_w,
    gain,
    grid_out,
    grid_table,
    latents,
    first_table,
    second_table,
    local_table,
    halo_out,
    receivers,
    base,
    terms_enc,
    terms_mesh,
    split_weight,
    sums,
    share_out,
    share_in,
    hidden,
    fetch_sem,
    send_sem,
    recv_sem,
):
    n_dom, n_feat = sizes
    dom = lax.axis_index("dom")
    feat = lax.axis_index("feat")
    sub = lax.axis_index("sub")
    width = base.shape[2]
    mesh_rows = latents.shape[2]
    tile_count = mesh_rows // TILE
    half_tiles = tile_count // 2
    half_rows = mesh_rows // 2
    chunks = half_tiles // CHUNK
    chunk_rows = CHUNK * TILE
    half_band = grid_half.shape[1]
    model_width = grid_half.shape[2]
    half_model = model_width // 2
    half_tile = TILE // 2
    half_units = half_band // half_tile

    tables = (first_table, second_table)
    fetches = []
    sends = []

    def fetch(source, target):
        copy = pltpu.make_async_copy(source, target, fetch_sem.at[len(fetches)])
        copy.start()
        fetches.append(copy)
        return copy

    def send(source, target, device):
        slot = len(sends)
        copy = pltpu.make_async_remote_copy(
            src_ref=source,
            dst_ref=target,
            send_sem=send_sem.at[slot],
            recv_sem=recv_sem.at[slot],
            device_id=device,
            device_id_type=DEVICE_MESH,
        )
        copy.start()
        sends.append(copy)
        return copy

    sibling = {"sub": 1 - sub}
    own_rows = pl.ds(pl.multiple_of(sub * half_rows, half_rows), half_rows)

    got_grid = fetch(
        grid_latent.at[:, pl.ds(pl.multiple_of(sub * half_band, half_band), half_band), :], grid_half
    )
    got_sender = fetch(sender_weight, sender_w)
    got_latent = fetch(mesh_latent, latents.at[0, feat])
    got_receiver = fetch(receiver_weight, receiver_w)
    got_node = fetch(node_weight, node_w)
    got_output = fetch(output_weight, output_w.at[feat])
    got_gain = fetch(norm_gain, gain.at[feat])
    got_rest = [
        fetch(far_encoder_geometry, encoder_geometry),
        fetch(far_edge_weight, edge_weight),
        fetch(far_edge_bias, edge_bias),
        fetch(far_mesh_geometry, mesh_geometry),
        fetch(far_encoder_lanes, encoder_lanes),
        fetch(far_mesh_lanes, mesh_lanes),
        fetch(far_node_bias, node_bias),
    ]

    barrier = pltpu.get_barrier_semaphore()
    dom_peers = [lax.rem(dom + step, n_dom) for step in range(1, n_dom)]
    feat_peers = [lax.rem(feat + step, n_feat) for step in range(1, n_feat)]
    feat_sources = [lax.rem(feat + n_feat - step, n_feat) for step in range(1, n_feat)]
    for peer in dom_peers:
        pl.semaphore_signal(barrier, inc=1, device_id={"dom": peer}, device_id_type=DEVICE_MESH)
    for peer in feat_peers:
        pl.semaphore_signal(barrier, inc=1, device_id={"feat": peer}, device_id_type=DEVICE_MESH)
    pl.semaphore_signal(barrier, inc=1, device_id=sibling, device_id_type=DEVICE_MESH)
    pl.semaphore_wait(barrier, n_dom + n_feat - 1)

    got_latent.wait()
    first_latents = [
        send(latents.at[0, feat, own_rows, :], latents.at[0, feat, own_rows, :], {"feat": peer})
        for peer in feat_peers
    ]

    got_grid.wait()
    got_sender.wait()

    def band_rows(source):
        return pl.ds(source * (2 * half_units) + sub * half_units, half_units)

    def project(peer):
        values = jnp.dot(grid_half[peer], sender_w[0], preferred_element_type=F32)
        return values.astype(BF16).reshape(half_units, half_tile, width)

    steps = sorted(range(1, n_dom), key=lambda step: -min(step, n_dom - step))
    grid_copies = []
    for step in steps:
        peer = lax.rem(dom + step, n_dom)
        grid_out[step - 1] = project(peer)
        grid_copies.append(
            send(grid_out.at[step - 1], grid_table.at[band_rows(dom)], {"dom": peer})
        )
    grid_table[band_rows(dom)] = project(dom)
    share_grid = [
        send(grid_table.at[band_rows(dom)], grid_table.at[band_rows(dom)], sibling)
    ]

    got_output.wait()
    got_gain.wait()
    model_half = pl.ds(pl.multiple_of(sub * half_model, half_model), half_model)
    weight_copies = []
    for layer in range(LAYERS):
        part = output_w.at[feat, layer, model_half, :]
        weight_copies.append([send(part, part, {"feat": peer}) for peer in feat_peers])
    gain_copies = [send(gain.at[feat], gain.at[feat], {"feat": peer}) for peer in feat_peers]

    def pieces(value):
        high = value.astype(BF16).astype(F32)
        middle = (value - high).astype(BF16).astype(F32)
        return high, middle, value - high - middle

    def split_geometry(geometry, target):
        high, middle, low = pieces(geometry[...])
        ones = jnp.ones((4, high.shape[1]), F32)
        target[...] = jnp.concatenate(
            [high, high, middle, middle, high, low, ones, 0.0 * ones], axis=0
        ).astype(BF16)

    for copy in got_rest:
        copy.wait()
    split_geometry(encoder_geometry, terms_enc)
    split_geometry(mesh_geometry, terms_mesh)
    for layer in range(LAYERS):
        high, middle, low = pieces(edge_weight[layer])
        bias = pieces(edge_bias[pl.ds(layer, 1), :])
        zeros = jnp.zeros((5, width), F32)
        split_weight[layer] = jnp.concatenate(
            [high, middle, high, middle, low, high, *bias, zeros], axis=0
        ).astype(BF16)

    share_first = []
    for source, copy in zip(feat_sources, first_latents):
        copy.wait_recv()
        part = latents.at[0, source, own_rows, :]
        share_first.append(send(part, part, sibling))

    got_receiver.wait()
    got_node.wait()
    for copy in share_first:
        copy.wait_recv()

    def whole(layer, rows):
        return jnp.concatenate([latents[layer, f, rows, :] for f in range(n_feat)], axis=1)

    def widen(layer):
        base[0] = jnp.dot(whole(layer, own_rows), node_w[layer], preferred_element_type=F32)
        receivers[...] = jnp.dot(
            whole(layer, slice(None)), receiver_w[layer], preferred_element_type=F32
        ).reshape(receivers.shape)

    widen(0)

    for step, copy in zip(steps, grid_copies):
        copy.wait_recv()
        source = lax.rem(dom + n_dom - step, n_dom)
        part = grid_table.at[band_rows(source)]
        share_grid.append(send(part, part, sibling))
    for copy in share_grid:
        copy.wait_recv()

    def edge_sums(layer, lanes, terms, load, row):
        blocks = 2 * lanes.shape[0]
        zero_slot = blocks
        sums[zero_slot] = jnp.zeros((TILE, width), F32)
        lane_at = lax.broadcasted_iota(jnp.int32, (1, 2 * TILE), 1)
        shift = jnp.where(lane_at >= TILE, TILE, 0)
        row_at = lax.broadcasted_iota(jnp.int32, (2 * TILE, 2 * TILE), 0)

        def body(pair, carry):
            rows = pl.ds(pl.multiple_of(pair * 2 * TILE, 2 * TILE), 2 * TILE)
            wanted = lanes[pl.ds(pair, 1), :] + shift
            chosen = jnp.where(row_at == wanted, 1.0, 0.0).astype(BF16)
            source = jnp.concatenate(
                [load(plan[row, 2 * pair]), load(plan[row, 2 * pair + 1]), split_weight[layer]],
                axis=0,
            )
            before = contract_rows(jnp.concatenate([chosen, terms[:, rows]], axis=0), source)
            for side in range(2):
                block = 2 * pair + side
                message = silu(
                    before[side * TILE : (side + 1) * TILE] + receivers[plan[row + 3, block]]
                )
                sums[block] = message + sums[plan[row + 1, block]]
            return carry

        lax.fori_loop(0, blocks // 2, body, 0, unroll=4)

    def load_grid(tile):
        return jnp.concatenate([grid_table[2 * tile], grid_table[2 * tile + 1]], axis=0)

    for layer in range(LAYERS):
        if layer == 0:
            edge_sums(0, encoder_lanes, terms_enc, load_grid, 0)
        else:
            senders = (
                jnp.dot(whole(layer, slice(None)), sender_w[layer], preferred_element_type=F32)
                .astype(BF16)
                .reshape(tile_count, TILE, width)
            )
            local_table[...] = senders
            tables[layer - 1][:tile_count] = senders
            table = tables[layer - 1]
            half = pl.ds(pl.multiple_of(sub * half_tile, half_tile), half_tile)
            halo_copies = []
            for way, step in enumerate((1, n_dom - 1, n_dom // 2)):
                peer = lax.rem(dom + step, n_dom)
                for slot in range(CAP):
                    listed = local_table[plan[8, CAP * way + slot]]
                    halo_out[layer - 1, way, slot] = jnp.where(
                        sub == 0, listed[:half_tile], listed[half_tile:]
                    )
                halo_copies.append(
                    send(
                        halo_out.at[layer - 1, way],
                        table.at[pl.ds(tile_count + CAP * way, CAP), half, :],
                        {"dom": peer},
                    )
                )
            widen(layer)
            share_halo = []
            for way, copy in enumerate(halo_copies):
                copy.wait_recv()
                part = table.at[pl.ds(tile_count + CAP * way, CAP), half, :]
                share_halo.append(send(part, part, sibling))
            for copy in share_halo:
                copy.wait_recv()
            edge_sums(layer, mesh_lanes, terms_mesh, lambda at: table[at], 4)

        ends = 2 if layer == 0 else 6
        sum_copies = []
        for c in range(chunks):
            for k in range(CHUNK * c, CHUNK * (c + 1)):
                share_out[layer, k] = sums[plan[ends, (1 - sub) * half_tiles + k]]
            part = pl.ds(CHUNK * c, CHUNK)
            sum_copies.append(send(share_out.at[layer, part], share_in.at[layer, part], sibling))
        for k in range(half_tiles):
            rows = slice(k * TILE, (k + 1) * TILE)
            base[0, rows, :] = base[0, rows, :] + sums[plan[ends, sub * half_tiles + k]]

        hidden_copies = []
        for c in range(chunks):
            rows = pl.ds(chunk_rows * c, chunk_rows)
            sum_copies[c].wait_recv()
            hidden[layer, feat, rows, :] = silu(
                base[0, rows, :]
                + share_in[layer, CHUNK * c : CHUNK * (c + 1)].reshape(chunk_rows, width)
                + node_bias[pl.ds(layer, 1), :]
            ).astype(BF16)
            part = hidden.at[layer, feat, rows, :]
            hidden_copies.append([send(part, part, {"feat": peer}) for peer in feat_peers])
        if layer == 0:
            share_weights = []
            for at in range(LAYERS):
                share_weights.append([])
                for source, copy in zip(feat_sources, weight_copies[at]):
                    copy.wait_recv()
                    part = output_w.at[source, at, model_half, :]
                    share_weights[at].append(send(part, part, sibling))
            for copy in gain_copies:
                copy.wait_recv()
        for copy in share_weights[layer]:
            copy.wait_recv()

        share_latent = []
        for c in range(chunks):
            rows = pl.ds(chunk_rows * c, chunk_rows)
            for copy in hidden_copies[c]:
                copy.wait_recv()
            whole_hidden = jnp.concatenate(
                [hidden[layer, f, rows, :] for f in range(n_feat)], axis=1
            )
            updates = [
                jnp.dot(whole_hidden, output_w[f, layer], preferred_element_type=F32)
                for f in range(n_feat)
            ]
            row_mean = sum(jnp.sum(u, axis=1, keepdims=True) for u in updates) / model_width
            row_squares = sum(jnp.sum(u * u, axis=1, keepdims=True) for u in updates) / model_width
            scale = lax.rsqrt(row_squares - row_mean * row_mean + EPSILON)
            mine = pl.ds(
                pl.multiple_of(sub * half_rows + c * chunk_rows, chunk_rows), chunk_rows
            )
            for f in range(n_feat):
                normed = (updates[f] - row_mean) * scale * gain[f, pl.ds(layer, 1), :]
                latents[layer + 1, f, mine, :] = (
                    latents[layer, f, mine, :].astype(F32) + normed
                ).astype(BF16)
            columns = pl.ds(0, n_feat) if layer < LAYERS - 1 else feat
            part = latents.at[layer + 1, columns, mine, :]
            share_latent.append(send(part, part, sibling))
        for copy in share_latent:
            copy.wait_recv()

    out[...] = latents[LAYERS, feat]
    for copy in sends:
        copy.wait_send()


def local(
    n_dom,
    n_feat,
    grid_latent,
    mesh_latent,
    encoder_tiles,
    encoder_lanes,
    encoder_geometry,
    halo_tiles,
    mesh_tiles,
    mesh_lanes,
    mesh_geometry,
    sender_weight,
    receiver_weight,
    node_weight,
    edge_weight,
    edge_bias,
    node_bias,
    output_weight,
    norm_gain,
):
    model, width = sender_weight.shape[1:]
    grid_rows = grid_latent.shape[0]
    mesh_rows = mesh_latent.shape[0]
    tile_count = mesh_rows // TILE
    band = grid_rows // n_dom
    enc_edges = encoder_lanes.shape[0]
    mesh_edges = mesh_lanes.shape[0]
    half_rows = mesh_rows // 2
    chunks = half_rows // (CHUNK * TILE)
    copies = 2 * n_dom + (n_feat - 1) * (3 + 2 * LAYERS + LAYERS * chunks)
    copies += 2 * LAYERS * chunks + 6 * (LAYERS - 1)
    smem = pl.BlockSpec(memory_space=pltpu.SMEM)
    plan = pl.pallas_call(
        functools.partial(plan_kernel, n_dom, tile_count),
        out_shape=jax.ShapeDtypeStruct((9, max(enc_edges, mesh_edges) // TILE), jnp.int32),
        in_specs=[smem] * 3,
        out_specs=smem,
        scratch_shapes=[pltpu.SMEM((tile_count,), jnp.int32)],
        compiler_params=pltpu.CompilerParams(vmem_limit_bytes=VMEM_GRANT),
    )(encoder_tiles, mesh_tiles, halo_tiles.transpose(2, 0, 1))
    vmem = pl.BlockSpec(memory_space=pltpu.VMEM)
    far = pl.BlockSpec(memory_space=pltpu.HBM)
    return pl.pallas_call(
        functools.partial(kernel, (n_dom, n_feat)),
        out_shape=jax.ShapeDtypeStruct((mesh_rows, width), BF16),
        in_specs=[smem] + [far] * 14,
        out_specs=vmem,
        scratch_shapes=[
            pltpu.VMEM((enc_edges // (2 * TILE), 2 * TILE), jnp.int32),
            pltpu.VMEM((mesh_edges // (2 * TILE), 2 * TILE), jnp.int32),
            pltpu.VMEM(encoder_geometry.shape, F32),
            pltpu.VMEM(mesh_geometry.shape, F32),
            pltpu.VMEM(edge_weight.shape, F32),
            pltpu.VMEM(edge_bias.shape, F32),
            pltpu.VMEM(node_bias.shape, F32),
            pltpu.VMEM((n_dom, band // 2, model), BF16),
            pltpu.VMEM((LAYERS, model, width), BF16),
            pltpu.VMEM((LAYERS, model, width), BF16),
            pltpu.VMEM((LAYERS, model, width), BF16),
            pltpu.VMEM((n_feat, LAYERS, model, width), BF16),
            pltpu.VMEM((n_feat, LAYERS, width), F32),
            pltpu.VMEM((n_dom - 1, band // TILE, TILE // 2, width), BF16),
            pltpu.VMEM((2 * grid_rows // TILE, TILE // 2, width), BF16),
            pltpu.VMEM((LAYERS + 1, n_feat, mesh_rows, width), BF16),
            pltpu.VMEM((tile_count + 3 * CAP, TILE, width), BF16),
            pltpu.VMEM((tile_count + 3 * CAP, TILE, width), BF16),
            pltpu.VMEM((tile_count, TILE, width), BF16),
            pltpu.VMEM((LAYERS - 1, 3, CAP, TILE // 2, width), BF16),
            pltpu.VMEM((tile_count, TILE, width), F32),
            pltpu.VMEM((1, half_rows, width), F32),
            pltpu.VMEM((SPLIT_ROWS, enc_edges), BF16),
            pltpu.VMEM((SPLIT_ROWS, mesh_edges), BF16),
            pltpu.VMEM((LAYERS, SPLIT_ROWS, width), BF16),
            pltpu.VMEM((max(enc_edges, mesh_edges) // TILE + 1, TILE, width), F32),
            pltpu.VMEM((LAYERS, tile_count // 2, TILE, width), F32),
            pltpu.VMEM((LAYERS, tile_count // 2, TILE, width), F32),
            pltpu.VMEM((LAYERS, n_feat, half_rows, width), BF16),
            pltpu.SemaphoreType.DMA((14,)),
            pltpu.SemaphoreType.DMA((copies,)),
            pltpu.SemaphoreType.DMA((copies,)),
        ],
        compiler_params=pltpu.CompilerParams(
            collective_id=0, has_side_effects=True, vmem_limit_bytes=VMEM_GRANT
        ),
    )(
        plan,
        encoder_lanes.reshape(-1, 2 * TILE),
        mesh_lanes.reshape(-1, 2 * TILE),
        encoder_geometry,
        mesh_geometry,
        edge_weight,
        edge_bias,
        node_bias,
        grid_latent.reshape(n_dom, band, model),
        mesh_latent,
        sender_weight,
        receiver_weight,
        node_weight,
        output_weight,
        norm_gain,
    )


def solution(mesh):
    in_specs = (
        P(("groups", "dom"), None),
        P(("groups", "dom"), "feat"),
        P(None, ("dom", "sub")),
        P(("dom", "sub")),
        P(None, ("dom", "sub")),
        P("dom", None, None),
        P(None, ("dom", "sub")),
        P(("dom", "sub")),
        P(None, ("dom", "sub")),
        P(None, None, "feat"),
        P(None, None, "feat"),
        P(None, None, "feat"),
        P(None, None, "feat"),
        P(None, "feat"),
        P(None, "feat"),
        P(None, None, "feat"),
        P(None, "feat"),
    )
    out_specs = P(("groups", "dom"), "feat")
    return jax.shard_map(
        functools.partial(local, mesh.shape["dom"], mesh.shape["feat"]),
        mesh=mesh,
        in_specs=in_specs,
        out_specs=out_specs,
        check_vma=False,
    )
```

```python
import functools

import jax
import jax.numpy as jnp
from jax import lax
from jax.experimental import pallas as pl
from jax.experimental.pallas import tpu as pltpu
from jax.sharding import PartitionSpec as P

TILE = 64
LAYERS = 3
CAP = 3
CHUNK = 2
SPLIT_ROWS = 32
EPSILON = 1e-05
VMEM_GRANT = 63 * 1024 * 1024
DEVICE_MESH = pl.DeviceIdType.MESH
F32 = jnp.float32
BF16 = jnp.bfloat16


def silu(value):
    half = 0.5 * value
    return half + half * jnp.tanh(half)


def contract_rows(left, right):
    return lax.dot_general(
        left, right, (((0,), (0,)), ((), ())), preferred_element_type=F32
    )


def kernel(
    sizes,
    encoder_tiles,
    mesh_tiles,
    halo_tiles,
    far_encoder_lanes,
    far_mesh_lanes,
    far_encoder_geometry,
    far_mesh_geometry,
    far_edge_weight,
    far_edge_bias,
    far_node_bias,
    grid_latent,
    mesh_latent,
    sender_weight,
    receiver_weight,
    node_weight,
    output_weight,
    norm_gain,
    out,
    plan,
    encoder_lanes,
    mesh_lanes,
    encoder_geometry,
    mesh_geometry,
    edge_weight,
    edge_bias,
    node_bias,
    grid_half,
    sender_w,
    receiver_w,
    node_w,
    output_w,
    gain,
    grid_out,
    grid_table,
    latents,
    first_table,
    second_table,
    local_table,
    halo_out,
    receivers,
    base,
    terms_enc,
    terms_mesh,
    split_weight,
    sums,
    share_out,
    share_in,
    hidden,
    fetch_sem,
    send_sem,
    recv_sem,
):
    n_dom, n_feat = sizes
    dom = lax.axis_index("dom")
    feat = lax.axis_index("feat")
    sub = lax.axis_index("sub")
    width = base.shape[2]
    mesh_rows = latents.shape[2]
    tile_count = mesh_rows // TILE
    half_tiles = tile_count // 2
    half_rows = mesh_rows // 2
    chunks = half_tiles // CHUNK
    chunk_rows = CHUNK * TILE
    half_band = grid_half.shape[1]
    model_width = grid_half.shape[2]
    half_model = model_width // 2
    half_tile = TILE // 2
    half_units = half_band // half_tile

    tables = (first_table, second_table)
    fetches = []
    sends = []

    def fetch(source, target):
        copy = pltpu.make_async_copy(source, target, fetch_sem.at[len(fetches)])
        copy.start()
        fetches.append(copy)
        return copy

    def send(source, target, device):
        slot = len(sends)
        copy = pltpu.make_async_remote_copy(
            src_ref=source,
            dst_ref=target,
            send_sem=send_sem.at[slot],
            recv_sem=recv_sem.at[slot],
            device_id=device,
            device_id_type=DEVICE_MESH,
        )
        copy.start()
        sends.append(copy)
        return copy

    sibling = {"sub": 1 - sub}
    own_rows = pl.ds(pl.multiple_of(sub * half_rows, half_rows), half_rows)

    got_grid = fetch(
        grid_latent.at[:, pl.ds(pl.multiple_of(sub * half_band, half_band), half_band), :], grid_half
    )
    got_sender = fetch(sender_weight, sender_w)
    got_latent = fetch(mesh_latent, latents.at[0, feat])
    got_receiver = fetch(receiver_weight, receiver_w)
    got_node = fetch(node_weight, node_w)
    got_output = fetch(output_weight, output_w.at[feat])
    got_gain = fetch(norm_gain, gain.at[feat])
    got_rest = [
        fetch(far_encoder_geometry, encoder_geometry),
        fetch(far_edge_weight, edge_weight),
        fetch(far_edge_bias, edge_bias),
        fetch(far_mesh_geometry, mesh_geometry),
        fetch(far_encoder_lanes, encoder_lanes),
        fetch(far_mesh_lanes, mesh_lanes),
        fetch(far_node_bias, node_bias),
    ]

    barrier = pltpu.get_barrier_semaphore()
    dom_peers = [lax.rem(dom + step, n_dom) for step in range(1, n_dom)]
    feat_peers = [lax.rem(feat + step, n_feat) for step in range(1, n_feat)]
    feat_sources = [lax.rem(feat + n_feat - step, n_feat) for step in range(1, n_feat)]
    for peer in dom_peers:
        pl.semaphore_signal(barrier, inc=1, device_id={"dom": peer}, device_id_type=DEVICE_MESH)
    for peer in feat_peers:
        pl.semaphore_signal(barrier, inc=1, device_id={"feat": peer}, device_id_type=DEVICE_MESH)
    pl.semaphore_signal(barrier, inc=1, device_id=sibling, device_id_type=DEVICE_MESH)
    pl.semaphore_wait(barrier, n_dom + n_feat - 1)

    got_latent.wait()
    first_latents = [
        send(latents.at[0, feat, own_rows, :], latents.at[0, feat, own_rows, :], {"feat": peer})
        for peer in feat_peers
    ]

    got_grid.wait()
    got_sender.wait()

    def band_rows(source):
        return pl.ds(source * (2 * half_units) + sub * half_units, half_units)

    def project(peer):
        values = jnp.dot(grid_half[peer], sender_w[0], preferred_element_type=F32)
        return values.astype(BF16).reshape(half_units, half_tile, width)

    steps = sorted(range(1, n_dom), key=lambda step: -min(step, n_dom - step))
    grid_copies = []
    for step in steps:
        peer = lax.rem(dom + step, n_dom)
        grid_out[step - 1] = project(peer)
        grid_copies.append(
            send(grid_out.at[step - 1], grid_table.at[band_rows(dom)], {"dom": peer})
        )
    grid_table[band_rows(dom)] = project(dom)
    share_grid = [
        send(grid_table.at[band_rows(dom)], grid_table.at[band_rows(dom)], sibling)
    ]

    got_output.wait()
    got_gain.wait()
    model_half = pl.ds(pl.multiple_of(sub * half_model, half_model), half_model)
    weight_copies = []
    for layer in range(LAYERS):
        part = output_w.at[feat, layer, model_half, :]
        weight_copies.append([send(part, part, {"feat": peer}) for peer in feat_peers])
    gain_copies = [send(gain.at[feat], gain.at[feat], {"feat": peer}) for peer in feat_peers]

    def chain(tiles, row, place):
        blocks = tiles.shape[1]

        def follow(block, last):
            target = tiles[1, block]
            earlier = last[0]
            for t in range(1, tile_count):
                earlier = jnp.where(target == t, last[t], earlier)
            plan[row, block] = place(tiles[0, block])
            plan[row + 1, block] = earlier
            plan[row + 3, block] = target
            return tuple(jnp.where(target == t, block, last[t]) for t in range(tile_count))

        last = lax.fori_loop(0, blocks, follow, (jnp.int32(blocks),) * tile_count)
        for t in range(tile_count):
            plan[row + 2, t] = last[t]

    ways = (1, n_dom - 1, n_dom // 2)

    def mesh_place(tile):
        place = tile
        for way, step in enumerate(ways):
            first = tile_count + CAP * lax.rem(dom + n_dom - step, n_dom)
            slot = tile - first
            listed = jnp.logical_and(slot >= 0, slot < CAP)
            place = jnp.where(listed, tile_count + CAP * way + slot, place)
        return place

    chain(encoder_tiles, 0, lambda tile: tile)
    chain(mesh_tiles, 4, mesh_place)
    for way, step in enumerate(ways):
        peer = lax.rem(dom + step, n_dom)
        for slot in range(CAP):
            plan[8, CAP * way + slot] = jnp.maximum(halo_tiles[slot, 0, peer], 0)

    def pieces(value):
        high = value.astype(BF16).astype(F32)
        middle = (value - high).astype(BF16).astype(F32)
        return high, middle, value - high - middle

    def split_geometry(geometry, target):
        high, middle, low = pieces(geometry[...])
        ones = jnp.ones((4, high.shape[1]), F32)
        target[...] = jnp.concatenate(
            [high, high, middle, middle, high, low, ones, 0.0 * ones], axis=0
        ).astype(BF16)

    for copy in got_rest:
        copy.wait()
    split_geometry(encoder_geometry, terms_enc)
    split_geometry(mesh_geometry, terms_mesh)
    for layer in range(LAYERS):
        high, middle, low = pieces(edge_weight[layer])
        bias = pieces(edge_bias[pl.ds(layer, 1), :])
        zeros = jnp.zeros((5, width), F32)
        split_weight[layer] = jnp.concatenate(
            [high, middle, high, middle, low, high, *bias, zeros], axis=0
        ).astype(BF16)

    share_first = []
    for source, copy in zip(feat_sources, first_latents):
        copy.wait_recv()
        part = latents.at[0, source, own_rows, :]
        share_first.append(send(part, part, sibling))

    got_receiver.wait()
    got_node.wait()
    for copy in share_first:
        copy.wait_recv()

    def whole(layer, rows):
        return jnp.concatenate([latents[layer, f, rows, :] for f in range(n_feat)], axis=1)

    def widen(layer):
        base[0] = jnp.dot(whole(layer, own_rows), node_w[layer], preferred_element_type=F32)
        receivers[...] = jnp.dot(
            whole(layer, slice(None)), receiver_w[layer], preferred_element_type=F32
        ).reshape(receivers.shape)

    widen(0)

    for step, copy in zip(steps, grid_copies):
        copy.wait_recv()
        source = lax.rem(dom + n_dom - step, n_dom)
        part = grid_table.at[band_rows(source)]
        share_grid.append(send(part, part, sibling))
    for copy in share_grid:
        copy.wait_recv()

    def edge_sums(layer, lanes, terms, load, row):
        blocks = 2 * lanes.shape[0]
        zero_slot = blocks
        sums[zero_slot] = jnp.zeros((TILE, width), F32)
        lane_at = lax.broadcasted_iota(jnp.int32, (1, 2 * TILE), 1)
        shift = jnp.where(lane_at >= TILE, TILE, 0)
        row_at = lax.broadcasted_iota(jnp.int32, (2 * TILE, 2 * TILE), 0)

        def body(pair, carry):
            rows = pl.ds(pl.multiple_of(pair * 2 * TILE, 2 * TILE), 2 * TILE)
            wanted = lanes[pl.ds(pair, 1), :] + shift
            chosen = jnp.where(row_at == wanted, 1.0, 0.0).astype(BF16)
            source = jnp.concatenate(
                [load(plan[row, 2 * pair]), load(plan[row, 2 * pair + 1]), split_weight[layer]],
                axis=0,
            )
            before = contract_rows(jnp.concatenate([chosen, terms[:, rows]], axis=0), source)
            for side in range(2):
                block = 2 * pair + side
                message = silu(
                    before[side * TILE : (side + 1) * TILE] + receivers[plan[row + 3, block]]
                )
                sums[block] = message + sums[plan[row + 1, block]]
            return carry

        lax.fori_loop(0, blocks // 2, body, 0, unroll=4)

    def load_grid(tile):
        return jnp.concatenate([grid_table[2 * tile], grid_table[2 * tile + 1]], axis=0)

    for layer in range(LAYERS):
        if layer == 0:
            edge_sums(0, encoder_lanes, terms_enc, load_grid, 0)
        else:
            senders = (
                jnp.dot(whole(layer, slice(None)), sender_w[layer], preferred_element_type=F32)
                .astype(BF16)
                .reshape(tile_count, TILE, width)
            )
            local_table[...] = senders
            tables[layer - 1][:tile_count] = senders
            table = tables[layer - 1]
            half = pl.ds(pl.multiple_of(sub * half_tile, half_tile), half_tile)
            halo_copies = []
            for way, step in enumerate(ways):
                peer = lax.rem(dom + step, n_dom)
                for slot in range(CAP):
                    listed = local_table[plan[8, CAP * way + slot]]
                    halo_out[layer - 1, way, slot] = jnp.where(
                        sub == 0, listed[:half_tile], listed[half_tile:]
                    )
                halo_copies.append(
                    send(
                        halo_out.at[layer - 1, way],
                        table.at[pl.ds(tile_count + CAP * way, CAP), half, :],
                        {"dom": peer},
                    )
                )
            widen(layer)
            share_halo = []
            for way, copy in enumerate(halo_copies):
                copy.wait_recv()
                part = table.at[pl.ds(tile_count + CAP * way, CAP), half, :]
                share_halo.append(send(part, part, sibling))
            for copy in share_halo:
                copy.wait_recv()
            edge_sums(layer, mesh_lanes, terms_mesh, lambda at: table[at], 4)

        ends = 2 if layer == 0 else 6
        sum_copies = []
        for c in range(chunks):
            for k in range(CHUNK * c, CHUNK * (c + 1)):
                share_out[layer, k] = sums[plan[ends, (1 - sub) * half_tiles + k]]
            part = pl.ds(CHUNK * c, CHUNK)
            sum_copies.append(send(share_out.at[layer, part], share_in.at[layer, part], sibling))
        for k in range(half_tiles):
            rows = slice(k * TILE, (k + 1) * TILE)
            base[0, rows, :] = base[0, rows, :] + sums[plan[ends, sub * half_tiles + k]]

        hidden_copies = []
        for c in range(chunks):
            rows = pl.ds(chunk_rows * c, chunk_rows)
            sum_copies[c].wait_recv()
            hidden[layer, feat, rows, :] = silu(
                base[0, rows, :]
                + share_in[layer, CHUNK * c : CHUNK * (c + 1)].reshape(chunk_rows, width)
                + node_bias[pl.ds(layer, 1), :]
            ).astype(BF16)
            part = hidden.at[layer, feat, rows, :]
            hidden_copies.append([send(part, part, {"feat": peer}) for peer in feat_peers])
        if layer == 0:
            share_weights = []
            for at in range(LAYERS):
                share_weights.append([])
                for source, copy in zip(feat_sources, weight_copies[at]):
                    copy.wait_recv()
                    part = output_w.at[source, at, model_half, :]
                    share_weights[at].append(send(part, part, sibling))
            for copy in gain_copies:
                copy.wait_recv()
        for copy in share_weights[layer]:
            copy.wait_recv()

        share_latent = []
        for c in range(chunks):
            rows = pl.ds(chunk_rows * c, chunk_rows)
            for copy in hidden_copies[c]:
                copy.wait_recv()
            whole_hidden = jnp.concatenate(
                [hidden[layer, f, rows, :] for f in range(n_feat)], axis=1
            )
            updates = [
                jnp.dot(whole_hidden, output_w[f, layer], preferred_element_type=F32)
                for f in range(n_feat)
            ]
            row_mean = sum(jnp.sum(u, axis=1, keepdims=True) for u in updates) / model_width
            row_squares = sum(jnp.sum(u * u, axis=1, keepdims=True) for u in updates) / model_width
            scale = lax.rsqrt(row_squares - row_mean * row_mean + EPSILON)
            mine = pl.ds(
                pl.multiple_of(sub * half_rows + c * chunk_rows, chunk_rows), chunk_rows
            )
            for f in range(n_feat):
                normed = (updates[f] - row_mean) * scale * gain[f, pl.ds(layer, 1), :]
                latents[layer + 1, f, mine, :] = (
                    latents[layer, f, mine, :].astype(F32) + normed
                ).astype(BF16)
            columns = pl.ds(0, n_feat) if layer < LAYERS - 1 else feat
            part = latents.at[layer + 1, columns, mine, :]
            share_latent.append(send(part, part, sibling))
        for copy in share_latent:
            copy.wait_recv()

    out[...] = latents[LAYERS, feat]
    for copy in sends:
        copy.wait_send()


def local(
    n_dom,
    n_feat,
    grid_latent,
    mesh_latent,
    encoder_tiles,
    encoder_lanes,
    encoder_geometry,
    halo_tiles,
    mesh_tiles,
    mesh_lanes,
    mesh_geometry,
    sender_weight,
    receiver_weight,
    node_weight,
    edge_weight,
    edge_bias,
    node_bias,
    output_weight,
    norm_gain,
):
    model, width = sender_weight.shape[1:]
    grid_rows = grid_latent.shape[0]
    mesh_rows = mesh_latent.shape[0]
    tile_count = mesh_rows // TILE
    band = grid_rows // n_dom
    enc_edges = encoder_lanes.shape[0]
    mesh_edges = mesh_lanes.shape[0]
    half_rows = mesh_rows // 2
    chunks = half_rows // (CHUNK * TILE)
    copies = 2 * n_dom + (n_feat - 1) * (3 + 2 * LAYERS + LAYERS * chunks)
    copies += 2 * LAYERS * chunks + 6 * (LAYERS - 1)
    smem = pl.BlockSpec(memory_space=pltpu.SMEM)
    vmem = pl.BlockSpec(memory_space=pltpu.VMEM)
    far = pl.BlockSpec(memory_space=pltpu.HBM)
    return pl.pallas_call(
        functools.partial(kernel, (n_dom, n_feat)),
        out_shape=jax.ShapeDtypeStruct((mesh_rows, width), BF16),
        in_specs=[smem] * 3 + [far] * 14,
        out_specs=vmem,
        scratch_shapes=[
            pltpu.SMEM((9, max(enc_edges, mesh_edges) // TILE), jnp.int32),
            pltpu.VMEM((enc_edges // (2 * TILE), 2 * TILE), jnp.int32),
            pltpu.VMEM((mesh_edges // (2 * TILE), 2 * TILE), jnp.int32),
            pltpu.VMEM(encoder_geometry.shape, F32),
            pltpu.VMEM(mesh_geometry.shape, F32),
            pltpu.VMEM(edge_weight.shape, F32),
            pltpu.VMEM(edge_bias.shape, F32),
            pltpu.VMEM(node_bias.shape, F32),
            pltpu.VMEM((n_dom, band // 2, model), BF16),
            pltpu.VMEM((LAYERS, model, width), BF16),
            pltpu.VMEM((LAYERS, model, width), BF16),
            pltpu.VMEM((LAYERS, model, width), BF16),
            pltpu.VMEM((n_feat, LAYERS, model, width), BF16),
            pltpu.VMEM((n_feat, LAYERS, width), F32),
            pltpu.VMEM((n_dom - 1, band // TILE, TILE // 2, width), BF16),
            pltpu.VMEM((2 * grid_rows // TILE, TILE // 2, width), BF16),
            pltpu.VMEM((LAYERS + 1, n_feat, mesh_rows, width), BF16),
            pltpu.VMEM((tile_count + 3 * CAP, TILE, width), BF16),
            pltpu.VMEM((tile_count + 3 * CAP, TILE, width), BF16),
            pltpu.VMEM((tile_count, TILE, width), BF16),
            pltpu.VMEM((LAYERS - 1, 3, CAP, TILE // 2, width), BF16),
            pltpu.VMEM((tile_count, TILE, width), F32),
            pltpu.VMEM((1, half_rows, width), F32),
            pltpu.VMEM((SPLIT_ROWS, enc_edges), BF16),
            pltpu.VMEM((SPLIT_ROWS, mesh_edges), BF16),
            pltpu.VMEM((LAYERS, SPLIT_ROWS, width), BF16),
            pltpu.VMEM((max(enc_edges, mesh_edges) // TILE + 1, TILE, width), F32),
            pltpu.VMEM((LAYERS, tile_count // 2, TILE, width), F32),
            pltpu.VMEM((LAYERS, tile_count // 2, TILE, width), F32),
            pltpu.VMEM((LAYERS, n_feat, half_rows, width), BF16),
            pltpu.SemaphoreType.DMA((14,)),
            pltpu.SemaphoreType.DMA((copies,)),
            pltpu.SemaphoreType.DMA((copies,)),
        ],
        compiler_params=pltpu.CompilerParams(
            collective_id=0, has_side_effects=True, vmem_limit_bytes=VMEM_GRANT
        ),
    )(
        encoder_tiles,
        mesh_tiles,
        halo_tiles.transpose(2, 0, 1),
        encoder_lanes.reshape(-1, 2 * TILE),
        mesh_lanes.reshape(-1, 2 * TILE),
        encoder_geometry,
        mesh_geometry,
        edge_weight,
        edge_bias,
        node_bias,
        grid_latent.reshape(n_dom, band, model),
        mesh_latent,
        sender_weight,
        receiver_weight,
        node_weight,
        output_weight,
        norm_gain,
    )


def solution(mesh):
    in_specs = (
        P(("groups", "dom"), None),
        P(("groups", "dom"), "feat"),
        P(None, ("dom", "sub")),
        P(("dom", "sub")),
        P(None, ("dom", "sub")),
        P("dom", None, None),
        P(None, ("dom", "sub")),
        P(("dom", "sub")),
        P(None, ("dom", "sub")),
        P(None, None, "feat"),
        P(None, None, "feat"),
        P(None, None, "feat"),
        P(None, None, "feat"),
        P(None, "feat"),
        P(None, "feat"),
        P(None, None, "feat"),
        P(None, "feat"),
    )
    out_specs = P(("groups", "dom"), "feat")
    return jax.shard_map(
        functools.partial(local, mesh.shape["dom"], mesh.shape["feat"]),
        mesh=mesh,
        in_specs=in_specs,
        out_specs=out_specs,
        check_vma=False,
    )
```
